32 devices in a mesh: pair: 8 (over y, x, core), rep: 4 (over z).
Axes of the slice: x: 2, y: 2, z: 4, core: 2. Of those that a mesh axis runs over, the one named last changes fastest.
Arguments:
- amplitudes: bfloat16 [256, 4096], P('pair', 'rep'), may hold values from -6 to 6
- integrals: bfloat16 [4096, 4096], P('rep', 'pair'), may hold values from -0.25 to 0.25
- vir_offsets: int32 [9], replicated, may hold values from 0 to 4096, as said below
- vir_energy: float32 [4096], replicated, may hold values from 0.5 to 4
- occ_energy: float32 [256], P(('pair', 'rep')), may hold values from -3 to -0.3
Outputs:
- update: float32 [256, 4096], P(('pair', 'rep'))
The draws below stay inside these ranges and needn't reach their ends.
Inputs may be any that keep to these rules, and one draw needn't show every extreme that they name: Entries never fall, the first is 0 and the last 4096; irrep g holds the virtual pairs vir_offsets[g] to vir_offsets[g + 1] - 1, and no irrep is empty.
All inputs are finite; a program needn't handle non-finite values.
Results may differ from the reference program's by a relative error of at most 0.0003.
Values may be sent and summed in bfloat16 or wider, within the bound.
A program may use at most 192 MiB of HBM per device.

```python
import math
import jax
import jax.numpy as jnp
from jax import lax

AB_TILE = 512
OP = 256
VP = 4096
N_PAIR = 8


def draw_vir_offsets(key, part):
    key = jax.random.fold_in(key, 11)
    weights = jax.random.randint(key, (8,), 1, 9).astype(jnp.int32)
    running = jnp.cumsum(weights).astype(jnp.int32)
    inner = running * VP // running[7]
    return jnp.concatenate([jnp.zeros((1,), jnp.int32), inner.astype(jnp.int32)])


def steps_of(key, extent, cuts, least, high):
    def one(dim, blocks):
        steps = jax.random.uniform(jax.random.fold_in(jax.random.fold_in(key, 6), dim), (blocks,), jnp.float32, least / len(cuts), high / len(cuts))
        return jnp.repeat(jnp.exp(steps), extent[dim] // blocks).reshape((-1,) + (1,) * (len(extent) - dim - 1))

    loudness = one(*cuts[0])
    for cut in cuts[1:]:
        loudness = loudness * one(*cut)
    return loudness


def scatter_about(rng, dims, deviation, reach, shards=(), kind=jnp.bfloat16):
    factor_of = steps_of(rng, dims, shards, -0.22, 0.18) if shards else 1.0
    array = jax.random.normal(rng, dims, jnp.float32) * deviation * factor_of
    return jnp.minimum(jnp.maximum(array, -reach), reach).astype(kind)


def setup_inputs(seed: int = 0) -> dict:
    streams_of = jax.random.split(jax.random.key(seed), 6)
    return {
        "amplitudes": scatter_about(streams_of[0], (OP, VP), 1.0, 6.0, ((0, 8), (1, 4))),
        "integrals": scatter_about(streams_of[1], (VP, VP), (VP // 8) ** -0.5, 0.25, ((0, 4), (1, 8))),
        "vir_offsets": draw_vir_offsets(jax.random.fold_in(streams_of[5], 71), 0),
        "vir_energy": jnp.clip(jnp.exp(jax.random.uniform(streams_of[3], (VP,), jnp.float32, math.log(0.5), math.log(4.0))), 0.5, 4.0),
        "occ_energy": jnp.clip(-3.0 + 2.7 * jax.random.uniform(streams_of[4], (OP,), jnp.float32) ** steps_of(streams_of[4], (OP,), ((0, 32),), -0.2, 0.2), -3.0, -0.3),
    }


def irrep_of(indices, vir_offsets):
    return jnp.sum((indices[:, None] >= vir_offsets[None, 1:8]).astype(jnp.int32), axis=1)


def reference(amplitudes, integrals, vir_offsets, vir_energy, occ_energy):
    pair_ids = jnp.arange(VP, dtype=jnp.int32)
    row_irrep = irrep_of(pair_ids, vir_offsets)

    def one_tile(tile_index):
        first_col = (tile_index * AB_TILE).astype(jnp.int32)
        columns = lax.dynamic_slice_in_dim(integrals, first_col, AB_TILE, 1)
        col_irrep = lax.dynamic_slice_in_dim(row_irrep, first_col, AB_TILE, 0)
        same_irrep = row_irrep[:, None] == col_irrep[None, :]
        masked = jnp.where(same_irrep, columns, jnp.zeros_like(columns))
        return jnp.dot(amplitudes, masked, preferred_element_type=jnp.float32)

    tile_blocks = lax.map(one_tile, jnp.arange(N_PAIR, dtype=jnp.int32))
    ladder = jnp.transpose(tile_blocks, (1, 0, 2)).reshape(amplitudes.shape[0], VP)
    return ladder / (vir_energy[None, :] - occ_energy[:, None])
```

```python
import functools
import math

import jax
import jax.numpy as jnp
from jax import lax
from jax.experimental import pallas as pl
from jax.experimental.pallas import tpu as pltpu
from jax.sharding import PartitionSpec as P

MESH = pl.DeviceIdType.MESH


def kernel(n, R, amp_ref, int_ref, off_ref, ve_ref, occ_ref, out_ref,
           amp_all, masked, part, rs_buf, red, fin,
           load_sem, ag_send, ag_recv, rs_send, rs_recv, fin_send, fin_recv):
    p = lax.axis_index("pair")
    r = lax.axis_index("rep")
    rows, K = amp_ref.shape
    cols = int_ref.shape[1]
    m = rows // R
    chips = n // 2
    X = math.isqrt(chips)
    Y = chips // X
    core = p % 2
    cx = (p // 2) % X
    cy = p // 2 // X

    def peer(t, sign):
        s = t + 1
        o = s // 2
        x = (cx + X + sign * (o % X)) % X
        y = (cy + 2 * Y + sign * (o // X)) % Y
        return (y * X + x) * 2 + (core + (s + 1) % 2) % 2

    barrier = pltpu.get_barrier_semaphore()

    def greet(i, c):
        pl.semaphore_signal(barrier, inc=1, device_id=((p + i) % n, r), device_id_type=MESH)
        return c
    lax.fori_loop(1, n, greet, 0)
    for i in range(1, R):
        pl.semaphore_signal(barrier, inc=1, device_id=(p, (r + i) % R), device_id_type=MESH)

    load = pltpu.make_async_copy(int_ref, masked, load_sem)
    load.start()
    amp_all[p] = amp_ref[...]

    col = lax.broadcasted_iota(jnp.int32, (8, cols), 1) + p * cols
    lo = jnp.zeros((8, cols), jnp.int32)
    hi = jnp.full((8, cols), n * cols, jnp.int32)
    for g in range(1, 8):
        edge = off_ref[g]
        lo = jnp.where(col >= edge, jnp.maximum(lo, edge), lo)
        hi = jnp.where(col < edge, jnp.minimum(hi, edge), hi)
    lo = lo[:1] - r * K
    hi = hi[:1] - r * K
    load.wait()

    step = 128

    def mask_rows(i, c):
        at = pl.ds(pl.multiple_of(i * step, step), step)
        row = lax.broadcasted_iota(jnp.int32, (step, cols), 0) + i * step
        block = masked[at, :]
        keep = (row >= lo) & (row < hi)
        masked[at, :] = jnp.where(keep, block, jnp.zeros_like(block))
        return c
    lax.fori_loop(0, K // step, mask_rows, 0)

    pl.semaphore_wait(barrier, n - 1 + R - 1)

    def gather_copy(to):
        return pltpu.make_async_remote_copy(
            src_ref=amp_ref, dst_ref=amp_all.at[p], send_sem=ag_send.at[to], recv_sem=ag_recv.at[p],
            device_id=(to, r), device_id_type=MESH)

    def gather_from(q):
        return pltpu.make_async_remote_copy(
            src_ref=amp_ref, dst_ref=amp_all.at[q], send_sem=ag_send.at[q], recv_sem=ag_recv.at[q],
            device_id=(q, r), device_id_type=MESH)

    def send_amp(t, c):
        gather_copy(peer(t, -1)).start()
        return c
    lax.fori_loop(1, n, send_amp, 0)

    def sum_copy(q, to, slot):
        return pltpu.make_async_remote_copy(
            src_ref=part.at[q, to], dst_ref=rs_buf.at[q, slot], send_sem=rs_send.at[q, to],
            recv_sem=rs_recv.at[q, slot], device_id=(p, to), device_id_type=MESH)

    def multiply(t, c):
        q = peer(t, 1)

        @pl.when(t > 0)
        def _():
            gather_from(q).wait_recv()
        d = jnp.dot(amp_all[q], masked[...], preferred_element_type=jnp.float32)
        for k in range(R):
            part[q, k] = d[k * m:(k + 1) * m]
        for i in range(1, R):
            sum_copy(q, (r + i) % R, r).start()
        return c
    lax.fori_loop(0, n, multiply, 0)

    def final_copy(to, slot):
        return pltpu.make_async_remote_copy(
            src_ref=red.at[to], dst_ref=fin.at[slot], send_sem=fin_send.at[to], recv_sem=fin_recv.at[slot],
            device_id=(to, r), device_id_type=MESH)

    def reduce(t, c):
        q = peer(t, 1)
        total = part[q, r]
        for i in range(1, R):
            k = (r + i) % R
            sum_copy(q, k, k).wait_recv()
            total = total + rs_buf[q, k]

        @pl.when(t == 0)
        def _():
            fin[p] = total

        @pl.when(t > 0)
        def _():
            red[q] = total
            final_copy(q, p).start()
        return c
    lax.fori_loop(0, n, reduce, 0)

    which = lax.broadcasted_iota(jnp.int32, (m, cols), 0)
    occ = jnp.zeros((m, cols), jnp.float32)
    for i in range(m):
        occ = jnp.where(which == i, occ_ref[i], occ)

    def finish(t, c):
        q = peer(t, 1)

        @pl.when(t > 0)
        def _():
            final_copy(q, q).wait_recv()
        at = pl.ds(pl.multiple_of(q * cols, cols), cols)
        out_ref[:, at] = fin[q] / (ve_ref[:, at] - occ)
        return c
    lax.fori_loop(0, n, finish, 0)

    def drain(t, c):
        q = peer(t, 1)

        @pl.when(t > 0)
        def _():
            gather_from(q).wait_send()
            final_copy(q, p).wait_send()
        for i in range(1, R):
            sum_copy(q, (r + i) % R, r).wait_send()
        return c
    lax.fori_loop(0, n, drain, 0)


def per_device(n, R, amplitudes, integrals, vir_offsets, vir_energy, occ_energy):
    rows, K = amplitudes.shape
    cols = integrals.shape[1]
    m = rows // R
    vmem = pl.BlockSpec(memory_space=pltpu.VMEM)
    smem = pl.BlockSpec(memory_space=pltpu.SMEM)
    dma = pltpu.SemaphoreType.DMA
    return pl.pallas_call(
        functools.partial(kernel, n, R),
        out_shape=jax.ShapeDtypeStruct((m, n * cols), jnp.float32),
        in_specs=[vmem, pl.BlockSpec(memory_space=pl.ANY), smem, vmem, smem],
        out_specs=vmem,
        scratch_shapes=[
            pltpu.VMEM((n, rows, K), jnp.bfloat16),
            pltpu.VMEM((K, cols), jnp.bfloat16),
            pltpu.VMEM((n, R, m, cols), jnp.float32),
            pltpu.VMEM((n, R, m, cols), jnp.float32),
            pltpu.VMEM((n, m, cols), jnp.float32),
            pltpu.VMEM((n, m, cols), jnp.float32),
            dma, dma((n,)), dma((n,)), dma((n, R)), dma((n, R)), dma((n,)), dma((n,)),
        ],
        compiler_params=pltpu.CompilerParams(
            collective_id=0, has_side_effects=True, vmem_limit_bytes=40 * 1024 * 1024),
        cost_estimate=pl.CostEstimate(
            flops=2 * n * rows * K * cols, bytes_accessed=2 * K * cols, transcendentals=0),
    )(amplitudes, integrals, vir_offsets, vir_energy.reshape(1, -1), occ_energy)


def solution(mesh):
    placed = (P("pair", "rep"), P("rep", "pair"), P(), P(), P(("pair", "rep")))
    return jax.shard_map(
        functools.partial(per_device, mesh.shape["pair"], mesh.shape["rep"]),
        mesh=mesh, in_specs=placed, out_specs=P(("pair", "rep"), None), check_vma=False
    )
```

```python
import functools
import math

import jax
import jax.numpy as jnp
from jax import lax
from jax.experimental import pallas as pl
from jax.experimental.pallas import tpu as pltpu
from jax.sharding import PartitionSpec as P

MESH = pl.DeviceIdType.MESH


def kernel(n, R, amp_ref, int_ref, off_hbm, ve_hbm, occ_hbm, out_ref,
           amp_all, masked, part, rs_buf, red, fin, ve_ref, off_ref, occ_ref,
           load_sem, ag_send, ag_recv, rs_send, rs_recv, fin_send, fin_recv):
    p = lax.axis_index("pair")
    r = lax.axis_index("rep")
    rows, K = amp_ref.shape
    cols = int_ref.shape[1]
    m = rows // R
    chips = n // 2
    X = math.isqrt(chips)
    Y = chips // X
    core = p % 2
    cx = (p // 2) % X
    cy = p // 2 // X

    def peer(t, sign):
        s = t + 1
        o = s // 2
        x = (cx + X + sign * (o % X)) % X
        y = (cy + 2 * Y + sign * (o // X)) % Y
        return (y * X + x) * 2 + (core + (s + 1) % 2) % 2

    barrier = pltpu.get_barrier_semaphore()

    def greet(i, c):
        pl.semaphore_signal(barrier, inc=1, device_id=((p + i) % n, r), device_id_type=MESH)
        return c
    lax.fori_loop(1, n, greet, 0)
    for i in range(1, R):
        pl.semaphore_signal(barrier, inc=1, device_id=(p, (r + i) % R), device_id_type=MESH)

    offsets_load = pltpu.make_async_copy(off_hbm, off_ref, load_sem.at[0])
    load = pltpu.make_async_copy(int_ref, masked, load_sem.at[1])
    own_load = pltpu.make_async_copy(amp_ref, amp_all.at[p], load_sem.at[2])
    virtual_load = pltpu.make_async_copy(ve_hbm, ve_ref, load_sem.at[3])
    occupied_load = pltpu.make_async_copy(occ_hbm, occ_ref, load_sem.at[4])
    offsets_load.start()
    load.start()
    own_load.start()
    virtual_load.start()
    occupied_load.start()
    offsets_load.wait()

    col = lax.broadcasted_iota(jnp.int32, (8, cols), 1) + p * cols
    lo = jnp.zeros((8, cols), jnp.int32)
    hi = jnp.full((8, cols), n * cols, jnp.int32)
    for g in range(1, 8):
        edge = off_ref[g]
        lo = jnp.where(col >= edge, jnp.maximum(lo, edge), lo)
        hi = jnp.where(col < edge, jnp.minimum(hi, edge), hi)
    lo = lo[:1] - r * K
    hi = hi[:1] - r * K
    pl.semaphore_wait(barrier, n - 1 + R - 1)

    def gather_copy(to):
        return pltpu.make_async_remote_copy(
            src_ref=amp_ref, dst_ref=amp_all.at[p], send_sem=ag_send.at[to], recv_sem=ag_recv.at[p],
            device_id=(to, r), device_id_type=MESH)

    def gather_from(q):
        return pltpu.make_async_remote_copy(
            src_ref=amp_ref, dst_ref=amp_all.at[q], send_sem=ag_send.at[q], recv_sem=ag_recv.at[q],
            device_id=(q, r), device_id_type=MESH)

    def send_amp(t, c):
        gather_copy(peer(t, -1)).start()
        return c
    lax.fori_loop(1, n, send_amp, 0)

    load.wait()

    step = 128

    def mask_rows(i, c):
        at = pl.ds(pl.multiple_of(i * step, step), step)
        row = lax.broadcasted_iota(jnp.int32, (step, cols), 0) + i * step
        block = masked[at, :]
        keep = (row >= lo) & (row < hi)
        masked[at, :] = jnp.where(keep, block, jnp.zeros_like(block))
        return c
    lax.fori_loop(0, K // step, mask_rows, 0)

    own_load.wait()

    def sum_copy(q, to, slot):
        return pltpu.make_async_remote_copy(
            src_ref=part.at[q, to], dst_ref=rs_buf.at[q, slot], send_sem=rs_send.at[q, to],
            recv_sem=rs_recv.at[q, slot], device_id=(p, to), device_id_type=MESH)

    def multiply(t, c):
        q = peer(t, 1)

        @pl.when(t > 0)
        def _():
            gather_from(q).wait_recv()
        d = jnp.dot(amp_all[q], masked[...], preferred_element_type=jnp.float32)
        for k in range(R):
            part[q, k] = d[k * m:(k + 1) * m]
        for i in range(1, R):
            sum_copy(q, (r + i) % R, r).start()
        return c
    lax.fori_loop(0, n, multiply, 0)

    def final_copy(to, slot):
        return pltpu.make_async_remote_copy(
            src_ref=red.at[to], dst_ref=fin.at[slot], send_sem=fin_send.at[to], recv_sem=fin_recv.at[slot],
            device_id=(to, r), device_id_type=MESH)

    def reduce(t, c):
        q = peer(t, 1)
        total = part[q, r]
        for i in range(1, R):
            k = (r + i) % R
            sum_copy(q, k, k).wait_recv()
            total = total + rs_buf[q, k]

        @pl.when(t == 0)
        def _():
            fin[p] = total

        @pl.when(t > 0)
        def _():
            red[q] = total
            final_copy(q, p).start()
        return c
    lax.fori_loop(0, n, reduce, 0)

    virtual_load.wait()
    occupied_load.wait()
    which = lax.broadcasted_iota(jnp.int32, (m, cols), 0)
    occ = jnp.zeros((m, cols), jnp.float32)
    for i in range(m):
        occ = jnp.where(which == i, occ_ref[i], occ)

    def finish(t, c):
        q = peer(t, 1)

        @pl.when(t > 0)
        def _():
            final_copy(q, q).wait_recv()
        at = pl.ds(pl.multiple_of(q * cols, cols), cols)
        out_ref[:, at] = fin[q] / (ve_ref[:, at] - occ)
        return c
    lax.fori_loop(0, n, finish, 0)

    def drain(t, c):
        q = peer(t, 1)

        @pl.when(t > 0)
        def _():
            gather_from(q).wait_send()
            final_copy(q, p).wait_send()
        for i in range(1, R):
            sum_copy(q, (r + i) % R, r).wait_send()
        return c
    lax.fori_loop(0, n, drain, 0)


def per_device(n, R, amplitudes, integrals, vir_offsets, vir_energy, occ_energy):
    rows, K = amplitudes.shape
    cols = integrals.shape[1]
    m = rows // R
    vmem = pl.BlockSpec(memory_space=pltpu.VMEM)
    dma = pltpu.SemaphoreType.DMA
    return pl.pallas_call(
        functools.partial(kernel, n, R),
        out_shape=jax.ShapeDtypeStruct((m, n * cols), jnp.float32),
        in_specs=[pl.BlockSpec(memory_space=pltpu.HBM)] * 5,
        out_specs=vmem,
        scratch_shapes=[
            pltpu.VMEM((n, rows, K), jnp.bfloat16),
            pltpu.VMEM((K, cols), jnp.bfloat16),
            pltpu.VMEM((n, R, m, cols), jnp.float32),
            pltpu.VMEM((n, R, m, cols), jnp.float32),
            pltpu.VMEM((n, m, cols), jnp.float32),
            pltpu.VMEM((n, m, cols), jnp.float32),
            pltpu.VMEM((1, n * cols), jnp.float32),
            pltpu.SMEM(vir_offsets.shape, jnp.int32),
            pltpu.SMEM(occ_energy.shape, jnp.float32),
            dma((5,)), dma((n,)), dma((n,)), dma((n, R)), dma((n, R)), dma((n,)), dma((n,)),
        ],
        compiler_params=pltpu.CompilerParams(
            collective_id=0, has_side_effects=True, vmem_limit_bytes=56 * 1024 * 1024),
        cost_estimate=pl.CostEstimate(
            flops=2 * n * rows * K * cols, bytes_accessed=2 * K * cols, transcendentals=0),
    )(amplitudes, integrals, vir_offsets, vir_energy.reshape(1, -1), occ_energy)


def solution(mesh):
    placed = (P("pair", "rep"), P("rep", "pair"), P(), P(), P(("pair", "rep")))
    return jax.shard_map(
        functools.partial(per_device, mesh.shape["pair"], mesh.shape["rep"]),
        mesh=mesh, in_specs=placed, out_specs=P(("pair", "rep"), None), check_vma=False
    )
```

```python
import functools
import math

import jax
import jax.numpy as jnp
from jax import lax
from jax.experimental import pallas as pl
from jax.experimental.pallas import tpu as pltpu
from jax.sharding import PartitionSpec as P

MESH = pl.DeviceIdType.MESH


def kernel(n, R, amp_ref, int_ref, off_hbm, ve_hbm, occ_hbm, out_ref,
           amp_all, masked, part, rs_buf, red, fin, ve_ref, off_ref, occ_ref,
           load_sem, ag_send, ag_recv, rs_send, rs_recv, fin_send, fin_recv):
    p = lax.axis_index("pair")
    r = lax.axis_index("rep")
    rows, K = amp_ref.shape
    cols = int_ref.shape[1]
    m = rows // R
    chips = n // 2
    X = math.isqrt(chips)
    Y = chips // X
    core = p % 2
    cx = (p // 2) % X
    cy = p // 2 // X

    def peer(t, sign):
        s = t + 1
        o = s // 2
        x = (cx + X + sign * (o % X)) % X
        y = (cy + 2 * Y + sign * (o // X)) % Y
        return (y * X + x) * 2 + (core + (s + 1) % 2) % 2

    barrier = pltpu.get_barrier_semaphore()

    def greet(i, c):
        pl.semaphore_signal(barrier, inc=1, device_id=((p + i) % n, r), device_id_type=MESH)
        return c
    lax.fori_loop(1, n, greet, 0)
    for i in range(1, R):
        pl.semaphore_signal(barrier, inc=1, device_id=(p, (r + i) % R), device_id_type=MESH)

    offsets_load = pltpu.make_async_copy(off_hbm, off_ref, load_sem.at[0])
    load = pltpu.make_async_copy(int_ref, masked, load_sem.at[1])
    own_load = pltpu.make_async_copy(amp_ref, amp_all.at[p], load_sem.at[2])
    virtual_load = pltpu.make_async_copy(ve_hbm, ve_ref, load_sem.at[3])
    occupied_load = pltpu.make_async_copy(occ_hbm, occ_ref, load_sem.at[4])
    offsets_load.start()
    load.start()
    own_load.start()
    virtual_load.start()
    occupied_load.start()
    offsets_load.wait()

    col = lax.broadcasted_iota(jnp.int32, (8, cols), 1) + p * cols
    lo = jnp.zeros((8, cols), jnp.int32)
    hi = jnp.full((8, cols), n * cols, jnp.int32)
    for g in range(1, 8):
        edge = off_ref[g]
        lo = jnp.where(col >= edge, jnp.maximum(lo, edge), lo)
        hi = jnp.where(col < edge, jnp.minimum(hi, edge), hi)
    lo = lo[:1] - r * K
    hi = hi[:1] - r * K
    pl.semaphore_wait(barrier, n - 1 + R - 1)

    def gather_copy(to):
        return pltpu.make_async_remote_copy(
            src_ref=amp_ref, dst_ref=amp_all.at[p], send_sem=ag_send.at[to], recv_sem=ag_recv.at[p],
            device_id=(to, r), device_id_type=MESH)

    def gather_from(q):
        return pltpu.make_async_remote_copy(
            src_ref=amp_ref, dst_ref=amp_all.at[q], send_sem=ag_send.at[q], recv_sem=ag_recv.at[q],
            device_id=(q, r), device_id_type=MESH)

    def send_amp(t, c):
        gather_copy(peer(t, -1)).start()
        return c
    lax.fori_loop(1, n, send_amp, 0)

    load.wait()

    step = 128

    def mask_rows(i, c):
        at = pl.ds(pl.multiple_of(i * step, step), step)
        row = lax.broadcasted_iota(jnp.int32, (step, cols), 0) + i * step
        block = masked[at, :]
        keep = (row >= lo) & (row < hi)
        masked[at, :] = jnp.where(keep, block, jnp.zeros_like(block))
        return c
    lax.fori_loop(0, K // step, mask_rows, 0)

    own_load.wait()

    def sum_copy(q, to, slot):
        return pltpu.make_async_remote_copy(
            src_ref=part.at[q, to], dst_ref=rs_buf.at[q, slot], send_sem=rs_send.at[q, to],
            recv_sem=rs_recv.at[q, slot], device_id=(p, to), device_id_type=MESH)

    fold = R == 4
    other = r + 1 - 2 * (r % 2)
    near = 2 - r // 2
    far = 3 - 3 * (r // 2)
    inner = (r + 1) // 2 == 1

    def fold_copy(q, piece, slot, to):
        return pltpu.make_async_remote_copy(
            src_ref=part.at[q, piece], dst_ref=rs_buf.at[q, slot], send_sem=rs_send.at[q, piece],
            recv_sem=rs_recv.at[q, slot], device_id=(p, to), device_id_type=MESH)

    def fold_start(q):
        @pl.when(inner)
        def _():
            fold_copy(q, other, 0, other).start()

        @pl.when(jnp.logical_not(inner))
        def _():
            fold_copy(q, far, 3, other).start()
            fold_copy(q, near, 2, other).start()
            fold_copy(q, other, 0, other).start()

    def relay(t):
        q = peer(t, 1)

        @pl.when(inner)
        def _():
            fold_copy(q, far, 3, far).wait_recv()
            part[q, far] = part[q, far] + rs_buf[q, 3]
            fold_copy(q, far, 1, far).start()
            fold_copy(q, near, 2, near).wait_recv()
            part[q, near] = part[q, near] + rs_buf[q, 2]
            fold_copy(q, near, 1, near).start()

    lag = 2

    def multiply(t, c):
        q = peer(t, 1)

        @pl.when(t > 0)
        def _():
            gather_from(q).wait_recv()
        d = jnp.dot(amp_all[q], masked[...], preferred_element_type=jnp.float32)
        for k in range(R):
            part[q, k] = d[k * m:(k + 1) * m]
        if fold:
            fold_start(q)

            @pl.when(t >= lag)
            def _():
                relay(t - lag)
        else:
            for i in range(1, R):
                sum_copy(q, (r + i) % R, r).start()
        return c
    lax.fori_loop(0, n, multiply, 0)

    def final_copy(to, slot):
        return pltpu.make_async_remote_copy(
            src_ref=red.at[to], dst_ref=fin.at[slot], send_sem=fin_send.at[to], recv_sem=fin_recv.at[slot],
            device_id=(to, r), device_id_type=MESH)

    def reduce(t, c):
        q = peer(t, 1)
        total = part[q, r]
        if fold:
            @pl.when(t < lag)
            def _():
                relay(n - lag + t)
            for slot in range(2):
                fold_copy(q, other, slot, other).wait_recv()
                total = total + rs_buf[q, slot]
        else:
            for i in range(1, R):
                k = (r + i) % R
                sum_copy(q, k, k).wait_recv()
                total = total + rs_buf[q, k]

        @pl.when(t == 0)
        def _():
            fin[p] = total

        @pl.when(t > 0)
        def _():
            red[q] = total
            final_copy(q, p).start()
        return c
    lax.fori_loop(0, n, reduce, 0)

    virtual_load.wait()
    occupied_load.wait()
    which = lax.broadcasted_iota(jnp.int32, (m, cols), 0)
    occ = jnp.zeros((m, cols), jnp.float32)
    for i in range(m):
        occ = jnp.where(which == i, occ_ref[i], occ)

    def finish(t, c):
        q = peer(t, 1)

        @pl.when(t > 0)
        def _():
            final_copy(q, q).wait_recv()
        at = pl.ds(pl.multiple_of(q * cols, cols), cols)
        out_ref[:, at] = fin[q] / (ve_ref[:, at] - occ)
        return c
    lax.fori_loop(0, n, finish, 0)

    def drain(t, c):
        q = peer(t, 1)

        @pl.when(t > 0)
        def _():
            gather_from(q).wait_send()
            final_copy(q, p).wait_send()
        for i in range(1, R):
            sum_copy(q, (r + i) % R, r).wait_send()
        return c
    lax.fori_loop(0, n, drain, 0)


def per_device(n, R, amplitudes, integrals, vir_offsets, vir_energy, occ_energy):
    rows, K = amplitudes.shape
    cols = integrals.shape[1]
    m = rows // R
    vmem = pl.BlockSpec(memory_space=pltpu.VMEM)
    dma = pltpu.SemaphoreType.DMA
    return pl.pallas_call(
        functools.partial(kernel, n, R),
        out_shape=jax.ShapeDtypeStruct((m, n * cols), jnp.float32),
        in_specs=[pl.BlockSpec(memory_space=pltpu.HBM)] * 5,
        out_specs=vmem,
        scratch_shapes=[
            pltpu.VMEM((n, rows, K), jnp.bfloat16),
            pltpu.VMEM((K, cols), jnp.bfloat16),
            pltpu.VMEM((n, R, m, cols), jnp.float32),
            pltpu.VMEM((n, R, m, cols), jnp.float32),
            pltpu.VMEM((n, m, cols), jnp.float32),
            pltpu.VMEM((n, m, cols), jnp.float32),
            pltpu.VMEM((1, n * cols), jnp.float32),
            pltpu.SMEM(vir_offsets.shape, jnp.int32),
            pltpu.SMEM(occ_energy.shape, jnp.float32),
            dma((5,)), dma((n,)), dma((n,)), dma((n, R)), dma((n, R)), dma((n,)), dma((n,)),
        ],
        compiler_params=pltpu.CompilerParams(
            collective_id=0, has_side_effects=True, vmem_limit_bytes=56 * 1024 * 1024),
        cost_estimate=pl.CostEstimate(
            flops=2 * n * rows * K * cols, bytes_accessed=2 * K * cols, transcendentals=0),
    )(amplitudes, integrals, vir_offsets, vir_energy.reshape(1, -1), occ_energy)


def solution(mesh):
    placed = (P("pair", "rep"), P("rep", "pair"), P(), P(), P(("pair", "rep")))
    return jax.shard_map(
        functools.partial(per_device, mesh.shape["pair"], mesh.shape["rep"]),
        mesh=mesh, in_specs=placed, out_specs=P(("pair", "rep"), None), check_vma=False
    )
```

```python
import functools
import math

import jax
import jax.numpy as jnp
from jax import lax
from jax.experimental import pallas as pl
from jax.experimental.pallas import tpu as pltpu
from jax.sharding import PartitionSpec as P

MESH = pl.DeviceIdType.MESH


def kernel(n, R, amp_ref, int_ref, off_hbm, ve_hbm, occ_hbm, out_ref,
           amp_all, masked, part, rs_buf, red, fin, ve_ref, off_ref, occ_ref,
           load_sem, ag_send, ag_recv, rs_send, rs_recv, fin_send, fin_recv):
    p = lax.axis_index("pair")
    r = lax.axis_index("rep")
    rows, K = amp_ref.shape
    cols = int_ref.shape[1]
    m = rows // R
    chips = n // 2
    X = math.isqrt(chips)
    Y = chips // X
    core = p % 2
    cx = (p // 2) % X
    cy = p // 2 // X

    def peer(t, sign):
        other_core = t // chips
        o = t - other_core * (chips - 1)
        x = (cx + X + sign * (o % X)) % X
        y = (cy + 2 * Y + sign * (o // X)) % Y
        return (y * X + x) * 2 + (core + other_core) % 2

    sibling = p + 1 - 2 * core

    barrier = pltpu.get_barrier_semaphore()

    def greet(i, c):
        pl.semaphore_signal(barrier, inc=1, device_id=((p + i) % n, r), device_id_type=MESH)
        return c
    lax.fori_loop(1, n, greet, 0)
    for i in range(1, R):
        pl.semaphore_signal(barrier, inc=1, device_id=(p, (r + i) % R), device_id_type=MESH)

    offsets_load = pltpu.make_async_copy(off_hbm, off_ref, load_sem.at[0])
    load = pltpu.make_async_copy(int_ref, masked, load_sem.at[1])
    own_load = pltpu.make_async_copy(amp_ref, amp_all.at[p], load_sem.at[2])
    virtual_load = pltpu.make_async_copy(ve_hbm, ve_ref, load_sem.at[3])
    occupied_load = pltpu.make_async_copy(occ_hbm, occ_ref, load_sem.at[4])
    offsets_load.start()
    load.start()
    own_load.start()
    virtual_load.start()
    occupied_load.start()
    offsets_load.wait()

    col = lax.broadcasted_iota(jnp.int32, (8, cols), 1) + p * cols
    lo = jnp.zeros((8, cols), jnp.int32)
    hi = jnp.full((8, cols), n * cols, jnp.int32)
    for g in range(1, 8):
        edge = off_ref[g]
        lo = jnp.where(col >= edge, jnp.maximum(lo, edge), lo)
        hi = jnp.where(col < edge, jnp.minimum(hi, edge), hi)
    lo = lo[:1] - r * K
    hi = hi[:1] - r * K
    pl.semaphore_wait(barrier, n - 1 + R - 1)

    def gather_copy(to):
        return pltpu.make_async_remote_copy(
            src_ref=amp_ref, dst_ref=amp_all.at[p], send_sem=ag_send.at[to], recv_sem=ag_recv.at[p],
            device_id=(to, r), device_id_type=MESH)

    def gather_from(q):
        return pltpu.make_async_remote_copy(
            src_ref=amp_ref, dst_ref=amp_all.at[q], send_sem=ag_send.at[q], recv_sem=ag_recv.at[q],
            device_id=(q, r), device_id_type=MESH)

    def send_amp(t, c):
        gather_copy(peer(t, -1)).start()
        return c
    lax.fori_loop(1, chips, send_amp, 0)
    gather_copy(sibling).start()

    def pass_on(q):
        return pltpu.make_async_remote_copy(
            src_ref=amp_all.at[q], dst_ref=amp_all.at[q], send_sem=ag_send.at[q + 1 - 2 * core],
            recv_sem=ag_recv.at[q], device_id=(sibling, r), device_id_type=MESH)

    load.wait()

    step = 128

    def mask_rows(i, c):
        at = pl.ds(pl.multiple_of(i * step, step), step)
        row = lax.broadcasted_iota(jnp.int32, (step, cols), 0) + i * step
        block = masked[at, :]
        keep = (row >= lo) & (row < hi)
        masked[at, :] = jnp.where(keep, block, jnp.zeros_like(block))
        return c
    lax.fori_loop(0, K // step, mask_rows, 0)

    own_load.wait()

    def sum_copy(q, to, slot):
        return pltpu.make_async_remote_copy(
            src_ref=part.at[q, to], dst_ref=rs_buf.at[q, slot], send_sem=rs_send.at[q, to],
            recv_sem=rs_recv.at[q, slot], device_id=(p, to), device_id_type=MESH)

    fold = R == 4
    other = r + 1 - 2 * (r % 2)
    near = 2 - r // 2
    far = 3 - 3 * (r // 2)
    inner = (r + 1) // 2 == 1

    def fold_copy(q, piece, slot, to):
        return pltpu.make_async_remote_copy(
            src_ref=part.at[q, piece], dst_ref=rs_buf.at[q, slot], send_sem=rs_send.at[q, piece],
            recv_sem=rs_recv.at[q, slot], device_id=(p, to), device_id_type=MESH)

    def fold_start(q):
        @pl.when(inner)
        def _():
            fold_copy(q, other, 0, other).start()

        @pl.when(jnp.logical_not(inner))
        def _():
            fold_copy(q, far, 3, other).start()
            fold_copy(q, near, 2, other).start()
            fold_copy(q, other, 0, other).start()

    def relay(t):
        q = peer(t, 1)

        @pl.when(inner)
        def _():
            fold_copy(q, far, 3, far).wait_recv()
            part[q, far] = part[q, far] + rs_buf[q, 3]
            fold_copy(q, far, 1, far).start()
            fold_copy(q, near, 2, near).wait_recv()
            part[q, near] = part[q, near] + rs_buf[q, 2]
            fold_copy(q, near, 1, near).start()

    lag = 2

    def multiply(t, c):
        q = peer(t, 1)

        @pl.when(t > 0)
        def _():
            gather_from(q).wait_recv()

        @pl.when((t > 0) & (t < chips))
        def _():
            pass_on(q).start()
        d = jnp.dot(amp_all[q], masked[...], preferred_element_type=jnp.float32)
        for k in range(R):
            part[q, k] = d[k * m:(k + 1) * m]
        if fold:
            fold_start(q)

            @pl.when(t >= lag)
            def _():
                relay(t - lag)
        else:
            for i in range(1, R):
                sum_copy(q, (r + i) % R, r).start()
        return c
    lax.fori_loop(0, n, multiply, 0)

    def final_copy(to, slot):
        return pltpu.make_async_remote_copy(
            src_ref=red.at[to], dst_ref=fin.at[slot], send_sem=fin_send.at[to], recv_sem=fin_recv.at[slot],
            device_id=(to, r), device_id_type=MESH)

    def reduce(t, c):
        q = peer(t, 1)
        total = part[q, r]
        if fold:
            @pl.when(t < lag)
            def _():
                relay(n - lag + t)
            for slot in range(2):
                fold_copy(q, other, slot, other).wait_recv()
                total = total + rs_buf[q, slot]
        else:
            for i in range(1, R):
                k = (r + i) % R
                sum_copy(q, k, k).wait_recv()
                total = total + rs_buf[q, k]

        @pl.when(t == 0)
        def _():
            fin[p] = total

        @pl.when(t > 0)
        def _():
            red[q] = total
            final_copy(q, p).start()
        return c
    lax.fori_loop(0, n, reduce, 0)

    virtual_load.wait()
    occupied_load.wait()
    which = lax.broadcasted_iota(jnp.int32, (m, cols), 0)
    occ = jnp.zeros((m, cols), jnp.float32)
    for i in range(m):
        occ = jnp.where(which == i, occ_ref[i], occ)

    def finish(t, c):
        q = peer(t, 1)

        @pl.when(t > 0)
        def _():
            final_copy(q, q).wait_recv()
        at = pl.ds(pl.multiple_of(q * cols, cols), cols)
        out_ref[:, at] = fin[q] / (ve_ref[:, at] - occ)
        return c
    lax.fori_loop(0, n, finish, 0)

    def drain(t, c):
        q = peer(t, 1)

        @pl.when(t > 0)
        def _():
            gather_from(q).wait_send()
            final_copy(q, p).wait_send()
        for i in range(1, R):
            sum_copy(q, (r + i) % R, r).wait_send()
        return c
    lax.fori_loop(0, n, drain, 0)


def per_device(n, R, amplitudes, integrals, vir_offsets, vir_energy, occ_energy):
    rows, K = amplitudes.shape
    cols = integrals.shape[1]
    m = rows // R
    vmem = pl.BlockSpec(memory_space=pltpu.VMEM)
    dma = pltpu.SemaphoreType.DMA
    return pl.pallas_call(
        functools.partial(kernel, n, R),
        out_shape=jax.ShapeDtypeStruct((m, n * cols), jnp.float32),
        in_specs=[pl.BlockSpec(memory_space=pltpu.HBM)] * 5,
        out_specs=vmem,
        scratch_shapes=[
            pltpu.VMEM((n, rows, K), jnp.bfloat16),
            pltpu.VMEM((K, cols), jnp.bfloat16),
            pltpu.VMEM((n, R, m, cols), jnp.float32),
            pltpu.VMEM((n, R, m, cols), jnp.float32),
            pltpu.VMEM((n, m, cols), jnp.float32),
            pltpu.VMEM((n, m, cols), jnp.float32),
            pltpu.VMEM((1, n * cols), jnp.float32),
            pltpu.SMEM(vir_offsets.shape, jnp.int32),
            pltpu.SMEM(occ_energy.shape, jnp.float32),
            dma((5,)), dma((n,)), dma((n,)), dma((n, R)), dma((n, R)), dma((n,)), dma((n,)),
        ],
        compiler_params=pltpu.CompilerParams(
            collective_id=0, has_side_effects=True, vmem_limit_bytes=56 * 1024 * 1024),
        cost_estimate=pl.CostEstimate(
            flops=2 * n * rows * K * cols, bytes_accessed=2 * K * cols, transcendentals=0),
    )(amplitudes, integrals, vir_offsets, vir_energy.reshape(1, -1), occ_energy)


def solution(mesh):
    placed = (P("pair", "rep"), P("rep", "pair"), P(), P(), P(("pair", "rep")))
    return jax.shard_map(
        functools.partial(per_device, mesh.shape["pair"], mesh.shape["rep"]),
        mesh=mesh, in_specs=placed, out_specs=P(("pair", "rep"), None), check_vma=False
    )
```

```python
import functools
import math

import jax
import jax.numpy as jnp
from jax import lax
from jax.experimental import pallas as pl
from jax.experimental.pallas import tpu as pltpu
from jax.sharding import PartitionSpec as P

MESH = pl.DeviceIdType.MESH


def kernel(n, R, amp_ref, int_ref, off_hbm, ve_hbm, occ_hbm, out_ref,
           amp_all, masked, part, rs_buf, red, fin, ve_ref, off_ref, occ_ref,
           load_sem, ag_send, ag_recv, rs_send, rs_recv, fin_send, fin_recv):
    p = lax.axis_index("pair")
    r = lax.axis_index("rep")
    rows, K = amp_ref.shape
    cols = int_ref.shape[1]
    m = rows // R
    chips = n // 2
    X = math.isqrt(chips)
    Y = chips // X
    core = p % 2
    cx = (p // 2) % X
    cy = p // 2 // X

    def peer(t, sign):
        other_core = t // chips
        o = t - other_core * (chips - 1)
        x = (cx + X + sign * (o % X)) % X
        y = (cy + 2 * Y + sign * (o // X)) % Y
        return (y * X + x) * 2 + (core + other_core) % 2

    sibling = p + 1 - 2 * core

    barrier = pltpu.get_barrier_semaphore()

    def greet(i, c):
        pl.semaphore_signal(barrier, inc=1, device_id=((p + i) % n, r), device_id_type=MESH)
        return c
    lax.fori_loop(1, n, greet, 0)
    for i in range(1, R):
        pl.semaphore_signal(barrier, inc=1, device_id=(p, (r + i) % R), device_id_type=MESH)

    offsets_load = pltpu.make_async_copy(off_hbm, off_ref, load_sem.at[0])
    load = pltpu.make_async_copy(int_ref, masked, load_sem.at[1])
    own_load = pltpu.make_async_copy(amp_ref, amp_all.at[p], load_sem.at[2])
    virtual_load = pltpu.make_async_copy(ve_hbm, ve_ref, load_sem.at[3])
    occupied_load = pltpu.make_async_copy(occ_hbm, occ_ref, load_sem.at[4])
    offsets_load.start()
    load.start()
    own_load.start()
    virtual_load.start()
    occupied_load.start()
    offsets_load.wait()

    col = lax.broadcasted_iota(jnp.int32, (8, cols), 1) + p * cols
    lo = jnp.zeros((8, cols), jnp.int32)
    hi = jnp.full((8, cols), n * cols, jnp.int32)
    for g in range(1, 8):
        edge = off_ref[g]
        lo = jnp.where(col >= edge, jnp.maximum(lo, edge), lo)
        hi = jnp.where(col < edge, jnp.minimum(hi, edge), hi)
    lo = lo[:1] - r * K
    hi = hi[:1] - r * K
    pl.semaphore_wait(barrier, n - 1 + R - 1)

    def gather_copy(to):
        return pltpu.make_async_remote_copy(
            src_ref=amp_ref, dst_ref=amp_all.at[p], send_sem=ag_send.at[to], recv_sem=ag_recv.at[p],
            device_id=(to, r), device_id_type=MESH)

    def gather_from(q):
        return pltpu.make_async_remote_copy(
            src_ref=amp_ref, dst_ref=amp_all.at[q], send_sem=ag_send.at[q], recv_sem=ag_recv.at[q],
            device_id=(q, r), device_id_type=MESH)

    def send_amp(t, c):
        gather_copy(peer(t, -1)).start()
        return c
    lax.fori_loop(1, chips, send_amp, 0)
    gather_copy(sibling).start()

    def pass_on(q):
        return pltpu.make_async_remote_copy(
            src_ref=amp_all.at[q], dst_ref=amp_all.at[q], send_sem=ag_send.at[q + 1 - 2 * core],
            recv_sem=ag_recv.at[q], device_id=(sibling, r), device_id_type=MESH)

    load.wait()

    step = 128

    def mask_rows(i, c):
        at = pl.ds(pl.multiple_of(i * step, step), step)
        row = lax.broadcasted_iota(jnp.int32, (step, cols), 0) + i * step
        block = masked[at, :]
        keep = (row >= lo) & (row < hi)
        masked[at, :] = jnp.where(keep, block, jnp.zeros_like(block))
        return c
    lax.fori_loop(0, K // step, mask_rows, 0)

    own_load.wait()

    def sum_copy(q, to, slot):
        return pltpu.make_async_remote_copy(
            src_ref=part.at[q, to], dst_ref=rs_buf.at[q, slot], send_sem=rs_send.at[q, to],
            recv_sem=rs_recv.at[q, slot], device_id=(p, to), device_id_type=MESH)

    def multiply(t, c):
        q = peer(t, 1)

        @pl.when(t > 0)
        def _():
            gather_from(q).wait_recv()

        @pl.when((t > 0) & (t < chips))
        def _():
            pass_on(q).start()
        d = jnp.dot(amp_all[q], masked[...], preferred_element_type=jnp.float32)
        for k in range(R):
            part[q, k] = d[k * m:(k + 1) * m]
        for i in range(1, R):
            sum_copy(q, (r + i) % R, r).start()
        return c

    def final_copy(to, slot):
        return pltpu.make_async_remote_copy(
            src_ref=red.at[to], dst_ref=fin.at[slot], send_sem=fin_send.at[to], recv_sem=fin_recv.at[slot],
            device_id=(to, r), device_id_type=MESH)

    def reduce(t, c):
        q = peer(t, 1)
        total = part[q, r]
        for i in range(1, R):
            k = (r + i) % R
            sum_copy(q, k, k).wait_recv()
            total = total + rs_buf[q, k]

        @pl.when(t == 0)
        def _():
            fin[p] = total

        @pl.when(t > 0)
        def _():
            red[q] = total
            final_copy(q, p).start()
        return c
    behind = 3

    def advance(t, c):
        @pl.when(t < n)
        def _():
            multiply(t, c)

        @pl.when(t >= behind)
        def _():
            reduce(t - behind, c)
        return c
    lax.fori_loop(0, n + behind, advance, 0)

    virtual_load.wait()
    occupied_load.wait()
    which = lax.broadcasted_iota(jnp.int32, (m, cols), 0)
    occ = jnp.zeros((m, cols), jnp.float32)
    for i in range(m):
        occ = jnp.where(which == i, occ_ref[i], occ)

    def finish(t, c):
        q = peer(t, 1)

        @pl.when(t > 0)
        def _():
            final_copy(q, q).wait_recv()
        at = pl.ds(pl.multiple_of(q * cols, cols), cols)
        out_ref[:, at] = fin[q] / (ve_ref[:, at] - occ)
        return c
    lax.fori_loop(0, n, finish, 0)

    def drain(t, c):
        q = peer(t, 1)

        @pl.when(t > 0)
        def _():
            gather_from(q).wait_send()
            final_copy(q, p).wait_send()
        for i in range(1, R):
            sum_copy(q, (r + i) % R, r).wait_send()
        return c
    lax.fori_loop(0, n, drain, 0)


def per_device(n, R, amplitudes, integrals, vir_offsets, vir_energy, occ_energy):
    rows, K = amplitudes.shape
    cols = integrals.shape[1]
    m = rows // R
    vmem = pl.BlockSpec(memory_space=pltpu.VMEM)
    dma = pltpu.SemaphoreType.DMA
    return pl.pallas_call(
        functools.partial(kernel, n, R),
        out_shape=jax.ShapeDtypeStruct((m, n * cols), jnp.float32),
        in_specs=[pl.BlockSpec(memory_space=pltpu.HBM)] * 5,
        out_specs=vmem,
        scratch_shapes=[
            pltpu.VMEM((n, rows, K), jnp.bfloat16),
            pltpu.VMEM((K, cols), jnp.bfloat16),
            pltpu.VMEM((n, R, m, cols), jnp.float32),
            pltpu.VMEM((n, R, m, cols), jnp.float32),
            pltpu.VMEM((n, m, cols), jnp.float32),
            pltpu.VMEM((n, m, cols), jnp.float32),
            pltpu.VMEM((1, n * cols), jnp.float32),
            pltpu.SMEM(vir_offsets.shape, jnp.int32),
            pltpu.SMEM(occ_energy.shape, jnp.float32),
            dma((5,)), dma((n,)), dma((n,)), dma((n, R)), dma((n, R)), dma((n,)), dma((n,)),
        ],
        compiler_params=pltpu.CompilerParams(
            collective_id=0, has_side_effects=True, vmem_limit_bytes=56 * 1024 * 1024),
        cost_estimate=pl.CostEstimate(
            flops=2 * n * rows * K * cols, bytes_accessed=2 * K * cols, transcendentals=0),
    )(amplitudes, integrals, vir_offsets, vir_energy.reshape(1, -1), occ_energy)


def solution(mesh):
    placed = (P("pair", "rep"), P("rep", "pair"), P(), P(), P(("pair", "rep")))
    return jax.shard_map(
        functools.partial(per_device, mesh.shape["pair"], mesh.shape["rep"]),
        mesh=mesh, in_specs=placed, out_specs=P(("pair", "rep"), None), check_vma=False
    )
```

```python
import functools
import math

import jax
import jax.numpy as jnp
from jax import lax
from jax.experimental import pallas as pl
from jax.experimental.pallas import tpu as pltpu
from jax.sharding import PartitionSpec as P

MESH = pl.DeviceIdType.MESH


def kernel(n, R, amp_ref, int_ref, off_hbm, ve_hbm, occ_hbm, out_ref,
           amp_all, masked, part, rs_buf, red, fin, ve_ref, off_ref, occ_ref, out_buf, out_sem,
           load_sem, ag_send, ag_recv, rs_send, rs_recv, fin_send, fin_recv):
    p = lax.axis_index("pair")
    r = lax.axis_index("rep")
    rows, K = amp_ref.shape
    cols = int_ref.shape[1]
    m = rows // R
    chips = n // 2
    X = math.isqrt(chips)
    Y = chips // X
    core = p % 2
    cx = (p // 2) % X
    cy = p // 2 // X

    def peer(t, sign):
        other_core = t // chips
        o = t - other_core * (chips - 1)
        x = (cx + X + sign * (o % X)) % X
        y = (cy + 2 * Y + sign * (o // X)) % Y
        return (y * X + x) * 2 + (core + other_core) % 2

    sibling = p + 1 - 2 * core

    barrier = pltpu.get_barrier_semaphore()

    def greet(i, c):
        pl.semaphore_signal(barrier, inc=1, device_id=((p + i) % n, r), device_id_type=MESH)
        return c
    lax.fori_loop(1, n, greet, 0)
    for i in range(1, R):
        pl.semaphore_signal(barrier, inc=1, device_id=(p, (r + i) % R), device_id_type=MESH)

    offsets_load = pltpu.make_async_copy(off_hbm, off_ref, load_sem.at[0])
    load = pltpu.make_async_copy(int_ref, masked, load_sem.at[1])
    own_load = pltpu.make_async_copy(amp_ref, amp_all.at[p], load_sem.at[2])
    virtual_load = pltpu.make_async_copy(ve_hbm, ve_ref, load_sem.at[3])
    occupied_load = pltpu.make_async_copy(occ_hbm, occ_ref, load_sem.at[4])
    offsets_load.start()
    load.start()
    own_load.start()
    virtual_load.start()
    occupied_load.start()
    offsets_load.wait()

    col = lax.broadcasted_iota(jnp.int32, (8, cols), 1) + p * cols
    lo = jnp.zeros((8, cols), jnp.int32)
    hi = jnp.full((8, cols), n * cols, jnp.int32)
    for g in range(1, 8):
        edge = off_ref[g]
        lo = jnp.where(col >= edge, jnp.maximum(lo, edge), lo)
        hi = jnp.where(col < edge, jnp.minimum(hi, edge), hi)
    lo = lo[:1] - r * K
    hi = hi[:1] - r * K
    pl.semaphore_wait(barrier, n - 1 + R - 1)

    def gather_copy(to):
        return pltpu.make_async_remote_copy(
            src_ref=amp_ref, dst_ref=amp_all.at[p], send_sem=ag_send.at[to], recv_sem=ag_recv.at[p],
            device_id=(to, r), device_id_type=MESH)

    def gather_from(q):
        return pltpu.make_async_remote_copy(
            src_ref=amp_ref, dst_ref=amp_all.at[q], send_sem=ag_send.at[q], recv_sem=ag_recv.at[q],
            device_id=(q, r), device_id_type=MESH)

    def send_amp(t, c):
        gather_copy(peer(t, -1)).start()
        return c
    lax.fori_loop(1, chips, send_amp, 0)
    gather_copy(sibling).start()

    def pass_on(q):
        return pltpu.make_async_remote_copy(
            src_ref=amp_all.at[q], dst_ref=amp_all.at[q], send_sem=ag_send.at[q + 1 - 2 * core],
            recv_sem=ag_recv.at[q], device_id=(sibling, r), device_id_type=MESH)

    load.wait()

    step = 128

    def mask_rows(i, c):
        at = pl.ds(pl.multiple_of(i * step, step), step)
        row = lax.broadcasted_iota(jnp.int32, (step, cols), 0) + i * step
        block = masked[at, :]
        keep = (row >= lo) & (row < hi)
        masked[at, :] = jnp.where(keep, block, jnp.zeros_like(block))
        return c
    lax.fori_loop(0, K // step, mask_rows, 0)

    own_load.wait()

    def sum_copy(q, to, slot):
        return pltpu.make_async_remote_copy(
            src_ref=part.at[q, to], dst_ref=rs_buf.at[q, slot], send_sem=rs_send.at[q, to],
            recv_sem=rs_recv.at[q, slot], device_id=(p, to), device_id_type=MESH)

    def multiply(t, c):
        q = peer(t, 1)

        @pl.when(t > 0)
        def _():
            gather_from(q).wait_recv()

        @pl.when((t > 0) & (t < chips))
        def _():
            pass_on(q).start()
        d = jnp.dot(amp_all[q], masked[...], preferred_element_type=jnp.float32)
        for k in range(R):
            part[q, k] = d[k * m:(k + 1) * m]
        for i in range(1, R):
            sum_copy(q, (r + i) % R, r).start()
        return c

    def final_copy(to, slot):
        return pltpu.make_async_remote_copy(
            src_ref=red.at[to], dst_ref=fin.at[slot], send_sem=fin_send.at[to], recv_sem=fin_recv.at[slot],
            device_id=(to, r), device_id_type=MESH)

    def reduce(t, c):
        q = peer(t, 1)
        total = part[q, r]
        for i in range(1, R):
            k = (r + i) % R
            sum_copy(q, k, k).wait_recv()
            total = total + rs_buf[q, k]

        @pl.when(t == 0)
        def _():
            fin[p] = total

        @pl.when(t > 0)
        def _():
            red[q] = total
            final_copy(q, p).start()
        return c
    behind = 3

    def advance(t, c):
        @pl.when(t < n)
        def _():
            multiply(t, c)

        @pl.when(t >= behind)
        def _():
            reduce(t - behind, c)
        return c
    lax.fori_loop(0, n + behind, advance, 0)

    virtual_load.wait()
    occupied_load.wait()
    which = lax.broadcasted_iota(jnp.int32, (m, cols), 0)
    occ = jnp.zeros((m, cols), jnp.float32)
    for i in range(m):
        occ = jnp.where(which == i, occ_ref[i], occ)

    def write_out(q):
        at = pl.ds(pl.multiple_of(q * cols, cols), cols)
        return pltpu.make_async_copy(out_buf.at[:, at], out_ref.at[:, at], out_sem.at[q])

    def finish(t, c):
        q = peer(t, 1)

        @pl.when(t > 0)
        def _():
            final_copy(q, q).wait_recv()
        at = pl.ds(pl.multiple_of(q * cols, cols), cols)
        out_buf[:, at] = fin[q] / (ve_ref[:, at] - occ)
        write_out(q).start()
        return c
    lax.fori_loop(0, n, finish, 0)

    def drain(t, c):
        q = peer(t, 1)
        write_out(q).wait()

        @pl.when(t > 0)
        def _():
            gather_from(q).wait_send()
            final_copy(q, p).wait_send()
        for i in range(1, R):
            sum_copy(q, (r + i) % R, r).wait_send()
        return c
    lax.fori_loop(0, n, drain, 0)


def per_device(n, R, amplitudes, integrals, vir_offsets, vir_energy, occ_energy):
    rows, K = amplitudes.shape
    cols = integrals.shape[1]
    m = rows // R
    dma = pltpu.SemaphoreType.DMA
    return pl.pallas_call(
        functools.partial(kernel, n, R),
        out_shape=jax.ShapeDtypeStruct((m, n * cols), jnp.float32),
        in_specs=[pl.BlockSpec(memory_space=pltpu.HBM)] * 5,
        out_specs=pl.BlockSpec(memory_space=pltpu.HBM),
        scratch_shapes=[
            pltpu.VMEM((n, rows, K), jnp.bfloat16),
            pltpu.VMEM((K, cols), jnp.bfloat16),
            pltpu.VMEM((n, R, m, cols), jnp.float32),
            pltpu.VMEM((n, R, m, cols), jnp.float32),
            pltpu.VMEM((n, m, cols), jnp.float32),
            pltpu.VMEM((n, m, cols), jnp.float32),
            pltpu.VMEM((1, n * cols), jnp.float32),
            pltpu.SMEM(vir_offsets.shape, jnp.int32),
            pltpu.SMEM(occ_energy.shape, jnp.float32),
            pltpu.VMEM((m, n * cols), jnp.float32),
            dma((n,)),
            dma((5,)), dma((n,)), dma((n,)), dma((n, R)), dma((n, R)), dma((n,)), dma((n,)),
        ],
        compiler_params=pltpu.CompilerParams(
            collective_id=0, has_side_effects=True, vmem_limit_bytes=56 * 1024 * 1024),
        cost_estimate=pl.CostEstimate(
            flops=2 * n * rows * K * cols, bytes_accessed=2 * K * cols, transcendentals=0),
    )(amplitudes, integrals, vir_offsets, vir_energy.reshape(1, -1), occ_energy)


def solution(mesh):
    placed = (P("pair", "rep"), P("rep", "pair"), P(), P(), P(("pair", "rep")))
    return jax.shard_map(
        functools.partial(per_device, mesh.shape["pair"], mesh.shape["rep"]),
        mesh=mesh, in_specs=placed, out_specs=P(("pair", "rep"), None), check_vma=False
    )
```

```python
import functools
import math

import jax
import jax.numpy as jnp
from jax import lax
from jax.experimental import pallas as pl
from jax.experimental.pallas import tpu as pltpu
from jax.sharding import PartitionSpec as P

MESH = pl.DeviceIdType.MESH


def kernel(n, R, amp_ref, int_ref, off_hbm, ve_hbm, occ_hbm, out_ref,
           amp_all, masked, part, rs_buf, red, fin, ve_ref, off_ref, occ_ref, out_buf, out_sem,
           load_sem, ag_send, ag_recv, rs_send, rs_recv, fin_send, fin_recv):
    p = lax.axis_index("pair")
    r = lax.axis_index("rep")
    rows, K = amp_ref.shape
    cols = int_ref.shape[1]
    m = rows // R
    chips = n // 2
    X = math.isqrt(chips)
    Y = chips // X
    core = p % 2
    cx = (p // 2) % X
    cy = p // 2 // X

    def peer(t, sign):
        other_core = t // chips
        o = t - other_core * (chips - 1)
        x = (cx + X + sign * (o % X)) % X
        y = (cy + 2 * Y + sign * (o // X)) % Y
        return (y * X + x) * 2 + (core + other_core) % 2

    sibling = p + 1 - 2 * core

    barrier = pltpu.get_barrier_semaphore()

    def greet(i, c):
        pl.semaphore_signal(barrier, inc=1, device_id=((p + i) % n, r), device_id_type=MESH)
        return c
    lax.fori_loop(1, n, greet, 0)
    for i in range(1, R):
        pl.semaphore_signal(barrier, inc=1, device_id=(p, (r + i) % R), device_id_type=MESH)

    offsets_load = pltpu.make_async_copy(off_hbm, off_ref, load_sem.at[0])
    load = pltpu.make_async_copy(int_ref, masked, load_sem.at[1])
    own_load = pltpu.make_async_copy(amp_ref, amp_all.at[p], load_sem.at[2])
    virtual_load = pltpu.make_async_copy(ve_hbm, ve_ref, load_sem.at[3])
    occupied_load = pltpu.make_async_copy(occ_hbm, occ_ref, load_sem.at[4])
    offsets_load.start()
    load.start()
    own_load.start()
    virtual_load.start()
    occupied_load.start()
    offsets_load.wait()

    col = lax.broadcasted_iota(jnp.int32, (8, cols), 1) + p * cols
    lo = jnp.zeros((8, cols), jnp.int32)
    hi = jnp.full((8, cols), n * cols, jnp.int32)
    for g in range(1, 8):
        edge = off_ref[g]
        lo = jnp.where(col >= edge, jnp.maximum(lo, edge), lo)
        hi = jnp.where(col < edge, jnp.minimum(hi, edge), hi)
    lo = lo[:1] - r * K
    hi = hi[:1] - r * K
    pl.semaphore_wait(barrier, n - 1 + R - 1)

    def gather_copy(to):
        return pltpu.make_async_remote_copy(
            src_ref=amp_ref, dst_ref=amp_all.at[p], send_sem=ag_send.at[to], recv_sem=ag_recv.at[p],
            device_id=(to, r), device_id_type=MESH)

    def gather_from(q):
        return pltpu.make_async_remote_copy(
            src_ref=amp_ref, dst_ref=amp_all.at[q], send_sem=ag_send.at[q], recv_sem=ag_recv.at[q],
            device_id=(q, r), device_id_type=MESH)

    def send_amp(t, c):
        gather_copy(peer(t, -1)).start()
        return c
    lax.fori_loop(1, chips, send_amp, 0)
    gather_copy(sibling).start()

    def pass_on(q):
        return pltpu.make_async_remote_copy(
            src_ref=amp_all.at[q], dst_ref=amp_all.at[q], send_sem=ag_send.at[q + 1 - 2 * core],
            recv_sem=ag_recv.at[q], device_id=(sibling, r), device_id_type=MESH)

    load.wait()

    step = 128

    def mask_rows(i, c):
        at = pl.ds(pl.multiple_of(i * step, step), step)
        row = lax.broadcasted_iota(jnp.int32, (step, cols), 0) + i * step
        block = masked[at, :]
        keep = (row >= lo) & (row < hi)
        masked[at, :] = jnp.where(keep, block, jnp.zeros_like(block))
        return c
    lax.fori_loop(0, K // step, mask_rows, 0)

    own_load.wait()

    def sum_copy(q, to, slot):
        return pltpu.make_async_remote_copy(
            src_ref=part.at[q, to], dst_ref=rs_buf.at[q, slot], send_sem=rs_send.at[q, to],
            recv_sem=rs_recv.at[q, slot], device_id=(p, to), device_id_type=MESH)

    def multiply(t, c):
        q = peer(t, 1)

        @pl.when(t > 0)
        def _():
            gather_from(q).wait_recv()

        @pl.when((t > 0) & (t < chips))
        def _():
            pass_on(q).start()
        d = jnp.dot(amp_all[q], masked[...], preferred_element_type=jnp.float32)
        for k in range(R):
            part[q, k] = d[k * m:(k + 1) * m]
        for i in range(1, R):
            sum_copy(q, (r + i) % R, r).start()
        return c

    def final_copy(to, slot):
        return pltpu.make_async_remote_copy(
            src_ref=red.at[to], dst_ref=fin.at[slot], send_sem=fin_send.at[to], recv_sem=fin_recv.at[slot],
            device_id=(to, r), device_id_type=MESH)

    def reduce(t, c):
        q = peer(t, 1)
        total = part[q, r]
        for i in range(1, R):
            k = (r + i) % R
            sum_copy(q, k, k).wait_recv()
            total = total + rs_buf[q, k]

        @pl.when(t == 0)
        def _():
            fin[p] = total

        @pl.when(t > 0)
        def _():
            red[q] = total
            final_copy(q, p).start()
        return c
    behind = 3

    def advance(t, c):
        @pl.when(t < n)
        def _():
            multiply(t, c)

        @pl.when(t >= behind)
        def _():
            reduce(t - behind, c)
        return c
    lax.fori_loop(0, n + behind, advance, 0)

    virtual_load.wait()
    occupied_load.wait()
    which = lax.broadcasted_iota(jnp.int32, (m, cols), 0)
    occ = jnp.zeros((m, cols), jnp.float32)
    for i in range(m):
        occ = jnp.where(which == i, occ_ref[i], occ)

    def drain_early(t, c):
        q = peer(t, 1)

        @pl.when(t > 0)
        def _():
            gather_from(q).wait_send()
        for i in range(1, R):
            sum_copy(q, (r + i) % R, r).wait_send()
        return c
    lax.fori_loop(0, n, drain_early, 0)

    def write_out(q):
        at = pl.ds(pl.multiple_of(q * cols, cols), cols)
        return pltpu.make_async_copy(out_buf.at[:, at], out_ref.at[:, at], out_sem.at[q])

    def finish(t, c):
        q = peer(t, 1)

        @pl.when(t > 0)
        def _():
            final_copy(q, q).wait_recv()
        at = pl.ds(pl.multiple_of(q * cols, cols), cols)
        out_buf[:, at] = fin[q] / (ve_ref[:, at] - occ)
        write_out(q).start()
        return c
    lax.fori_loop(0, n, finish, 0)

    def drain(t, c):
        q = peer(t, 1)
        write_out(q).wait()

        @pl.when(t > 0)
        def _():
            final_copy(q, p).wait_send()
        return c
    lax.fori_loop(0, n, drain, 0)


def per_device(n, R, amplitudes, integrals, vir_offsets, vir_energy, occ_energy):
    rows, K = amplitudes.shape
    cols = integrals.shape[1]
    m = rows // R
    dma = pltpu.SemaphoreType.DMA
    return pl.pallas_call(
        functools.partial(kernel, n, R),
        out_shape=jax.ShapeDtypeStruct((m, n * cols), jnp.float32),
        in_specs=[pl.BlockSpec(memory_space=pltpu.HBM)] * 5,
        out_specs=pl.BlockSpec(memory_space=pltpu.HBM),
        scratch_shapes=[
            pltpu.VMEM((n, rows, K), jnp.bfloat16),
            pltpu.VMEM((K, cols), jnp.bfloat16),
            pltpu.VMEM((n, R, m, cols), jnp.float32),
            pltpu.VMEM((n, R, m, cols), jnp.float32),
            pltpu.VMEM((n, m, cols), jnp.float32),
            pltpu.VMEM((n, m, cols), jnp.float32),
            pltpu.VMEM((1, n * cols), jnp.float32),
            pltpu.SMEM(vir_offsets.shape, jnp.int32),
            pltpu.SMEM(occ_energy.shape, jnp.float32),
            pltpu.VMEM((m, n * cols), jnp.float32),
            dma((n,)),
            dma((5,)), dma((n,)), dma((n,)), dma((n, R)), dma((n, R)), dma((n,)), dma((n,)),
        ],
        compiler_params=pltpu.CompilerParams(
            collective_id=0, has_side_effects=True, vmem_limit_bytes=56 * 1024 * 1024),
        cost_estimate=pl.CostEstimate(
            flops=2 * n * rows * K * cols, bytes_accessed=2 * K * cols, transcendentals=0),
    )(amplitudes, integrals, vir_offsets, vir_energy.reshape(1, -1), occ_energy)


def solution(mesh):
    placed = (P("pair", "rep"), P("rep", "pair"), P(), P(), P(("pair", "rep")))
    return jax.shard_map(
        functools.partial(per_device, mesh.shape["pair"], mesh.shape["rep"]),
        mesh=mesh, in_specs=placed, out_specs=P(("pair", "rep"), None), check_vma=False
    )
```
